32 devices in a mesh: ctx: 16 (over z, y, core), head: 2 (over x).
Axes of the slice: x: 2, y: 2, z: 4, core: 2. Of those that a mesh axis runs over, the one named last changes fastest.
Arguments:
- response_input: bfloat16 [64, 8192], P(('ctx', 'head')), may hold values from -6 to 6
- response_queries: bfloat16 [64, 8192], P(('ctx', 'head')), may hold values from -12 to 12
- response_keys: bfloat16 [64, 8192], P(('ctx', 'head')), may hold values from -6 to 6
- response_values: bfloat16 [64, 8192], P(('ctx', 'head')), may hold values from -6 to 6
- prompt_keys: bfloat16 [24576, 8192], P('ctx', 'head'), may hold values from -6 to 6
- prompt_values: bfloat16 [24576, 8192], P('ctx', 'head'), may hold values from -6 to 6
- query_down_weight: bfloat16 [8192, 16], replicated, may hold values from -0.0625 to 0.0625
- query_up_weight: bfloat16 [16, 8192], replicated, may hold values from -1.5 to 1.5
- value_down_weight: bfloat16 [8192, 16], replicated, may hold values from -0.0625 to 0.0625
- value_up_weight: bfloat16 [16, 8192], replicated, may hold values from -1.5 to 1.5
- response_index: int32 [64], replicated, may hold values from 0 to 7, never falling along the last dimension, each value on 1 to 16 neighbouring positions
Outputs:
- out_adapted: bfloat16 [64, 8192], P(('ctx', 'head'))
- out_base: bfloat16 [64, 8192], P(('ctx', 'head'))
The draws below stay inside these ranges and needn't reach their ends.
Inputs may be any that keep to these rules, and one draw needn't show every extreme that they name: `response_index`: never falls along the tokens; each response spans 1 to 16 tokens and one spans exactly 16.
All inputs are finite; a program needn't handle non-finite values.
Results may differ from the reference program's by a relative error of at most 0.0088.
Values may be sent and summed in bfloat16 or wider, within the bound.
A program may use at most 128 MiB of HBM per device.

```python
import math
import jax
import jax.numpy as jnp
import numpy as np
from jax import lax

HEADS = 64
HD = 128
ADAPTER_RANK = 16
RESPONSES = 8
CACHE_DEV = 1536
MODEL_WIDTH = 8192
QLEN = 64
CACHE = 24576
N_CTX = 16


def draw_response_queries(key, part):
    values = 2.8 * jax.random.truncated_normal(jax.random.fold_in(key, 1), -4.2, 4.2, (QLEN, MODEL_WIDTH), jnp.float32)
    return values.astype(jnp.bfloat16)


def draw_prompt_keys(key, part):
    values = jax.random.truncated_normal(jax.random.fold_in(key, 2), -6.0, 6.0, (CACHE, MODEL_WIDTH), jnp.float32)
    return values.astype(jnp.bfloat16)


def steps_of(key, extent, cuts, smallest, high):
    loudness = 1.0
    for position, shards_of in cuts:
        heights = jax.random.uniform(jax.random.fold_in(jax.random.fold_in(key, 6), position), (shards_of,), jnp.float32, smallest / len(cuts), high / len(cuts))
        loudness = loudness * jnp.repeat(jnp.exp(heights), extent[position] // shards_of).reshape((-1,) + (1,) * (len(extent) - 1 - position))
    return loudness


def length_profile(count, total, reach, skew):
    loads = [(1 << 20) // math.isqrt(standing ** skew) + 1 for standing in range(2, count + 1)]
    spare, given = total - reach - (count - 1), [1] * (count - 1)
    while spare > 0:
        free = [i for i in range(count - 1) if given[i] < reach]
        mass, budget = sum([loads[i] for i in free]), spare
        for i in free:
            more = min(reach - given[i], max(1, budget * loads[i] // mass), spare)
            given[i] = given[i] + more
            spare = spare - more
    return np.array([reach] + given)


def ragged(key, number_of, total, reach, skew):
    if number_of == 2:
        one = jax.random.randint(key, (), max(1, total - reach), min(reach, total - 1) + 1)
        return jnp.stack([one, total - one])
    lengths = jnp.asarray(length_profile(number_of, total, reach, skew), jnp.int32)
    twos = (number_of - 1) // 2
    source_of, sink = lengths[1:1 + 2 * twos:2], lengths[2:2 + 2 * twos:2]
    margin = jnp.minimum(source_of - 1, reach - sink)
    shifted = jax.random.randint(jax.random.fold_in(key, 1), (twos,), 0, 1 << 20) % (margin + 1)
    lengths = lengths.at[1:1 + 2 * twos:2].set(source_of - shifted).at[2:2 + 2 * twos:2].set(sink + shifted)
    return lengths[jax.random.permutation(jax.random.fold_in(key, 2), number_of)]


def centred(rng, dims, deviation, most, pieces=(), kind=jnp.bfloat16):
    gain = steps_of(rng, dims, pieces, -0.22, 0.18) if pieces else 1.0
    entries = jax.random.normal(rng, dims, jnp.float32) * deviation * gain
    return jnp.minimum(jnp.maximum(entries, -most), most).astype(kind)


def setup_inputs(seed: int = 0) -> dict:
    keys = jax.random.split(jax.random.key(seed), 12)
    response_input = centred(keys[0], (QLEN, MODEL_WIDTH), 1.0, 6.0, ((0, 32),))
    response_queries = draw_response_queries(jax.random.fold_in(keys[11], 71), 0)
    response_keys = centred(keys[2], (QLEN, MODEL_WIDTH), 1.0, 6.0, ((0, 32),))
    response_values = centred(keys[3], (QLEN, MODEL_WIDTH), 1.0, 6.0, ((0, 32),))
    prompt_keys = draw_prompt_keys(jax.random.fold_in(keys[11], 71), 0)
    prompt_values = centred(keys[5], (CACHE, MODEL_WIDTH), 1.0, 6.0, ((0, 16), (1, 2)))
    query_down_weight = centred(keys[6], (MODEL_WIDTH, ADAPTER_RANK), MODEL_WIDTH ** -0.5, 0.0625)
    query_up_weight = centred(keys[7], (ADAPTER_RANK, MODEL_WIDTH), ADAPTER_RANK ** -0.5, 1.5)
    value_down_weight = centred(keys[8], (MODEL_WIDTH, ADAPTER_RANK), MODEL_WIDTH ** -0.5, 0.0625)
    value_up_weight = centred(keys[9], (ADAPTER_RANK, MODEL_WIDTH), ADAPTER_RANK ** -0.5, 1.5)
    response_index = jnp.searchsorted(jnp.cumsum(ragged(keys[10], RESPONSES, QLEN, QLEN // 4, 1)), jnp.arange(QLEN), side="right").astype(jnp.int32)
    return dict(response_input=response_input, response_queries=response_queries, response_keys=response_keys, response_values=response_values, prompt_keys=prompt_keys, prompt_values=prompt_values, query_down_weight=query_down_weight, query_up_weight=query_up_weight, value_down_weight=value_down_weight, value_up_weight=value_up_weight, response_index=response_index)


def reference(response_input, response_queries, response_keys, response_values, prompt_keys, prompt_values, query_down_weight, query_up_weight, value_down_weight, value_up_weight, response_index):
    query_lowrank = jnp.dot(response_input, query_down_weight, preferred_element_type=jnp.float32).astype(jnp.bfloat16)
    value_lowrank = jnp.dot(response_input, value_down_weight, preferred_element_type=jnp.float32).astype(jnp.bfloat16)
    query_with_adapter = (response_queries.astype(jnp.float32) + jnp.dot(query_lowrank, query_up_weight, preferred_element_type=jnp.float32)).astype(jnp.bfloat16)
    value_with_adapter = (response_values.astype(jnp.float32) + jnp.dot(value_lowrank, value_up_weight, preferred_element_type=jnp.float32)).astype(jnp.bfloat16)
    queries = jnp.stack([query_with_adapter, response_queries], 1).reshape(QLEN, 2, HEADS, HD)
    stretch_values = jnp.stack([value_with_adapter, response_values], 1)
    shard_len = QLEN // N_CTX
    block_rows = 128 if QLEN % 128 == 0 else QLEN
    scale = HD ** -0.5

    def fold(running, shard_index):
        best, totals, weighted = running
        cache_start = (shard_index * CACHE_DEV).astype(jnp.int32)
        stretch_start = (shard_index * shard_len).astype(jnp.int32)
        key_rows = jnp.concatenate([lax.dynamic_slice_in_dim(prompt_keys, cache_start, CACHE_DEV, 0), lax.dynamic_slice_in_dim(response_keys, stretch_start, shard_len, 0)], 0)
        key_rows = key_rows.reshape(-1, HEADS, HD).astype(jnp.float32)
        cache_part = lax.dynamic_slice_in_dim(prompt_values, cache_start, CACHE_DEV, 0)
        value_rows = jnp.concatenate([jnp.stack([cache_part, cache_part], 1), lax.dynamic_slice_in_dim(stretch_values, stretch_start, shard_len, 0)], 0)
        value_rows = value_rows.reshape(-1, 2, HEADS, HD).astype(jnp.float32)
        key_pos = stretch_start + jnp.arange(shard_len, dtype=jnp.int32)
        key_seg = lax.dynamic_slice_in_dim(response_index, stretch_start, shard_len, 0)

        def one_block(block_index):
            start = (block_index * block_rows).astype(jnp.int32)
            query_block = lax.dynamic_slice_in_dim(queries, start, block_rows, 0).astype(jnp.float32)
            scores = jnp.einsum('qshd,khd->qshk', query_block, key_rows) * scale
            query_pos = start + jnp.arange(block_rows, dtype=jnp.int32)
            query_seg = lax.dynamic_slice_in_dim(response_index, start, block_rows, 0)
            stretch_ok = (key_pos[None, :] <= query_pos[:, None]) & (key_seg[None, :] == query_seg[:, None])
            visible = jnp.concatenate([jnp.ones((block_rows, CACHE_DEV), bool), stretch_ok], 1)
            scores = jnp.where(visible[:, None, None, :], scores, -jnp.inf)
            row_max = jnp.max(scores, -1)
            probs = jnp.exp(scores - row_max[..., None]).astype(jnp.bfloat16).astype(jnp.float32)
            part_total = jnp.sum(probs, -1)
            part_out = jnp.einsum('qshk,kshd->qshd', probs, value_rows)
            part_mean = lax.optimization_barrier((part_out / part_total[..., None]).astype(jnp.bfloat16)).astype(jnp.float32)
            return part_mean, part_total, row_max

        part_mean, part_total, part_max = lax.map(one_block, jnp.arange(QLEN // block_rows, dtype=jnp.int32))
        part_mean = part_mean.reshape(QLEN, 2, HEADS, HD)
        part_total = part_total.reshape(QLEN, 2, HEADS)
        part_max = part_max.reshape(QLEN, 2, HEADS)
        new_best = jnp.maximum(best, part_max)
        old_scale = jnp.exp(best - new_best)
        part_weight = part_total * jnp.exp(part_max - new_best)
        totals = totals * old_scale + part_weight
        weighted = weighted * old_scale[..., None] + part_mean * part_weight[..., None]
        return (new_best, totals, weighted), None

    initial = (jnp.full((QLEN, 2, HEADS), -jnp.inf, jnp.float32), jnp.zeros((QLEN, 2, HEADS), jnp.float32), jnp.zeros((QLEN, 2, HEADS, HD), jnp.float32))
    final, unused = lax.scan(fold, initial, jnp.arange(N_CTX, dtype=jnp.int32))
    result = (final[2] / final[1][..., None]).astype(jnp.bfloat16).reshape(QLEN, 2, HEADS * HD)
    return result[:, 0], result[:, 1]
```

```python
import functools

import jax
import jax.numpy as jnp
from jax import lax
from jax.experimental import pallas as pl
from jax.experimental.pallas import tpu as pltpu
from jax.sharding import PartitionSpec as P

HD = 128
LOG2E = 1.4426950408889634
F32 = jnp.float32
BF16 = jnp.bfloat16
MESH = pl.DeviceIdType.MESH


def dot(a, b):
    return jnp.dot(a, b, preferred_element_type=F32)


def dot_t(a, b):
    return lax.dot_general(a, b, (((1,), (1,)), ((), ())), preferred_element_type=F32)


def iota(shape, dim):
    return lax.broadcasted_iota(jnp.int32, shape, dim)


def kernel(
    n, g, tdev, steps,
    idx_ref, in_ref, q_ref, k_ref, v_ref, pk_hbm, pv_hbm, qd_ref, qu_ref, vd_ref, vu_ref,
    outa_ref, outb_ref,
    msgf, msg, kmsg, vmsg, gbuf, kx, vx, kbuf, vbuf, maskbuf, qbuf, kext, vext,
    obuf, rc, cbuf, ry, zbuf, rz, xbuf, rx,
    sem_kv, sx, rxs, sz, rzs, sy, rys, sc, rcs,
    scs, rcr, sys_, ryr, szs, rzr, sxs, rxr,
):
    c = lax.axis_index("ctx")
    h = lax.axis_index("head")
    nz = n // 4
    z = lax.div(c, 4)
    y = lax.rem(lax.div(c, 2), 2)
    core = lax.rem(c, 2)
    gw = pk_hbm.shape[1]
    chunks = 16 // tdev
    cjw = gw // chunks
    jper = chunks // steps
    cw = cjw * jper
    hc = cw // HD
    ng = n * g
    rows_slot = 2 * tdev
    rows = ng * rows_slot
    r1, r2 = rows // 2, rows // 4
    rc_rows = g * rows_slot
    fold = 1 if rc_rows >= 16 else 16 // rc_rows
    cache = pk_hbm.shape[0]
    blk = obuf.shape[1] if obuf.shape[1] < 128 else 128
    sb = blk // rows_slot
    nblk = rows // blk
    ext = g * rows_slot
    extp = kext.shape[1]
    tokens = ng * tdev

    def ctx_of(zz, yy, cc):
        return zz * 4 + yy * 2 + cc

    def slot_of(zz, yy, cc):
        return ((cc * 2 + yy) * nz + zz) * g

    def kv_copies(s):
        cols = pl.ds(s * cw, cw)
        return (
            pltpu.make_async_copy(pk_hbm.at[:, cols], kbuf.at[s], sem_kv.at[0, s]),
            pltpu.make_async_copy(pv_hbm.at[:, cols], vbuf.at[s], sem_kv.at[1, s]),
        )

    for s in range(steps):
        for cp in kv_copies(s):
            cp.start()

    barrier = pltpu.get_barrier_semaphore()
    sib = (ctx_of(z, y, 1 - core), h)
    ynb = (ctx_of(z, 1 - y, core), h)
    znb = [(ctx_of(lax.rem(z + d, nz), y, core), h) for d in range(1, nz)]
    xnb = [(c, lax.rem(h + d, g)) for d in range(1, g)]
    partners = [sib, ynb] + znb + xnb
    for p in partners:
        pl.semaphore_signal(barrier, inc=1, device_id=p, device_id_type=MESH)

    up_q = dot_t(in_ref[...], qd_ref[...])
    up_v = dot_t(in_ref[...], vd_ref[...])
    rank = up_q.shape[1]
    qf, kf, vf = (r[...].astype(F32) for r in (q_ref, k_ref, v_ref))
    msgf[...] = jnp.zeros(msgf.shape, F32)
    msgf[0:tdev, cjw:cjw + rank] = up_q
    msgf[tdev:2 * tdev, cjw:cjw + rank] = up_v
    for p in range(g):
        for src, dst in ((kf, kmsg), (vf, vmsg), (qf, msg)):
            for j in range(chunks):
                at = p * gw + j * cjw
                msgf[j * tdev:(j + 1) * tdev, 0:cjw] = src[:, at:at + cjw]
            if dst is msg:
                dst[p] = msgf[...].astype(BF16)
            else:
                dst[p] = msgf[:, 0:cjw].astype(BF16)

    pl.semaphore_wait(barrier, len(partners))

    my_slot = slot_of(z, y, core)

    def remote(src, dst, ss, rs, dev):
        return pltpu.make_async_remote_copy(
            src_ref=src, dst_ref=dst, send_sem=ss, recv_sem=rs, device_id=dev, device_id_type=MESH
        )

    gx = []
    for d in range(1, g):
        p = lax.rem(h + d, g)
        gx.append(remote(msg.at[p], gbuf.at[my_slot + h], sx.at[d, 0], rxs.at[d, 0], xnb[d - 1]))
        gx.append(remote(kmsg.at[p], kx.at[h], sx.at[d, 1], rxs.at[d, 1], xnb[d - 1]))
        gx.append(remote(vmsg.at[p], vx.at[h], sx.at[d, 2], rxs.at[d, 2], xnb[d - 1]))
    for cp in gx:
        cp.start()
    gbuf[my_slot + h] = msg[h]
    kx[h] = kmsg[h]
    vx[h] = vmsg[h]
    for cp in gx:
        cp.wait_recv()

    here = gbuf.at[pl.ds(my_slot, g)]
    gz = [remote(here, here, sz.at[d], rzs.at[d], znb[d - 1]) for d in range(1, nz)]
    for cp in gz:
        cp.start()

    def pick(rows_out, j, width, per):
        rr = iota((rows_out, width), 0)
        cc = iota((rows_out, width), 1)
        sl = lax.div(rr, per)
        return rr, cc, sl

    def ext_select(j):
        rr = iota((extp, g * 16), 0)
        cc = iota((extp, g * 16), 1)
        rem = lax.rem(rr, g * tdev)
        want = lax.div(rem, tdev) * 16 + j * tdev + lax.rem(rem, tdev)
        return jnp.where((cc == want) & (rr < ext), 1.0, 0.0).astype(BF16)

    own = gbuf[pl.ds(my_slot, g)].reshape(g * 16, cjw + HD)
    av = dot(ext_select(1), own[:, cjw:])
    av = jnp.where(iota((extp, HD), 0) < g * tdev, av, 0.0).astype(BF16)[:, 0:rank]
    kxa = kx[...].reshape(g * 16, cjw)
    vxa = vx[...].reshape(g * 16, cjw)
    group_at = pl.multiple_of(h * gw, gw)
    for j in range(chunks):
        sel = ext_select(j)
        s, lo = j // jper, (j % jper) * cjw
        kext[s, :, lo:lo + cjw] = dot(sel, kxa).astype(BF16)
        wv = vu_ref[:, pl.ds(pl.multiple_of(group_at + j * cjw, 128), cjw)]
        vext[s, :, lo:lo + cjw] = (dot(sel, vxa) + dot(av, wv)).astype(BF16)

    idx_row = idx_ref[...].astype(F32)
    eye = iota((tokens, tokens), 0) == iota((tokens, tokens), 1)
    idx_col = jnp.sum(jnp.where(eye, idx_row, 0.0), axis=1, keepdims=True)
    tok_u0 = c * (g * tdev) + lax.rem(iota((tokens, extp), 1), g * tdev)
    seg_u = jnp.sum(
        jnp.where(iota((tokens, extp), 0) == tok_u0, idx_col, 0.0), axis=0, keepdims=True
    )

    def row_tokens(shape, b):
        r = iota(shape, 0) + b * blk
        sl = lax.div(r, rows_slot)
        hh = lax.rem(sl, g)
        place = lax.div(sl, g)
        zz = lax.rem(place, nz)
        yc = lax.div(place, nz)
        ctx = zz * 4 + lax.rem(yc, 2) * 2 + lax.div(yc, 2)
        return (ctx * g + hh) * tdev + lax.rem(r, tdev), lax.rem(lax.div(r, tdev), 2)

    def mask_block(b, carry):
        tok_r, unused = row_tokens((blk, tokens), b)
        seg_r = jnp.sum(
            jnp.where(iota((blk, tokens), 1) == tok_r, idx_row, 0.0), axis=1, keepdims=True
        )
        tok, stream = row_tokens((blk, extp), b)
        u = iota((blk, extp), 1)
        tok_u = c * (g * tdev) + lax.rem(u, g * tdev)
        ok = (u < ext) & (lax.div(u, g * tdev) == stream) & (tok_u <= tok) & (seg_r == seg_u)
        maskbuf[pl.ds(pl.multiple_of(b * blk, blk), blk), :] = jnp.where(ok, 1.0, 0.0)
        return carry

    lax.fori_loop(0, nblk, mask_block, 0)

    for cp in gz:
        cp.wait_recv()
    half = gbuf.at[pl.ds((core * 2 + y) * (nz * g), nz * g)]
    gy = remote(half, half, sy.at[0], rys.at[0], ynb)
    gy.start()
    gy.wait_recv()
    side = gbuf.at[pl.ds(core * (2 * nz * g), 2 * nz * g)]
    gc = remote(side, side, sc.at[0], rcs.at[0], sib)
    gc.start()
    gc.wait_recv()

    def q_select(j):
        rr = iota((blk, sb * 16), 0)
        cc = iota((blk, sb * 16), 1)
        want = lax.div(rr, rows_slot) * 16 + j * tdev + lax.rem(rr, tdev)
        return jnp.where(cc == want, 1.0, 0.0).astype(BF16)

    def q_block(b, carry):
        x = gbuf[pl.ds(b * sb, sb)].reshape(sb * 16, cjw + HD)
        a = dot(q_select(0), x[:, cjw:])
        first = lax.rem(lax.div(iota((blk, HD), 0), tdev), 2) == 0
        a = jnp.where(first, a, 0.0).astype(BF16)[:, 0:rank]
        at = pl.ds(pl.multiple_of(b * blk, blk), blk)
        for j in range(chunks):
            wq = qu_ref[:, pl.ds(pl.multiple_of(group_at + j * cjw, 128), cjw)]
            s, lo = j // jper, (j % jper) * cjw
            qbuf[s, at, lo:lo + cjw] = (dot(q_select(j), x[:, 0:cjw]) + dot(a, wq)).astype(BF16)
        return carry

    lax.fori_loop(0, nblk, q_block, 0)

    scale2 = HD ** (-0.5) * LOG2E

    def pack_lse(cols_of, r):
        lane = iota((r, HD), 1)
        which = lax.rem(lane, hc)
        x = jnp.zeros((r, HD), F32)
        for i in range(hc):
            x = jnp.where(which == i, cols_of(i), x)
        hi = x.astype(BF16).astype(F32)
        mid = (x - hi).astype(BF16).astype(F32)
        lo = x - hi - mid
        x = jnp.where(lane < hc, hi, jnp.where(lane < 2 * hc, mid, lo))
        return jnp.where(lane < 3 * hc, x, 0.0)

    def spread(x):
        lane, col = iota((HD, cw), 0), iota((HD, cw), 1)
        e = (lax.rem(lane, hc) == lax.div(col, HD)) & (lane < 3 * hc)
        return dot(x.astype(BF16), jnp.where(e, 1.0, 0.0).astype(BF16))

    def merge(parts):
        ls = [spread(p[:, cw:]) for p in parts]
        top = functools.reduce(jnp.maximum, ls)
        ws = [jnp.exp2(x - top) for x in ls]
        den = functools.reduce(jnp.add, ws)
        num = functools.reduce(jnp.add, [w * p[:, 0:cw].astype(F32) for w, p in zip(ws, parts)])
        return num / den, top + jnp.log2(den)

    def compute(s):
        for cp in kv_copies(s):
            cp.wait()

        def block(b, carry):
            at = pl.ds(pl.multiple_of(b * blk, blk), blk)
            seen = maskbuf[at, :] > 0.5
            lses = []
            for i in range(hc):
                cols = slice(i * HD, (i + 1) * HD)
                q = qbuf[s, at, cols]
                sp = dot_t(q, kbuf[s, :, cols])
                se = jnp.where(seen, dot_t(q, kext[s, :, cols]), -jnp.inf)
                m = jnp.maximum(
                    jnp.max(sp, axis=1, keepdims=True), jnp.max(se, axis=1, keepdims=True)
                ) * scale2
                pp = jnp.exp2(sp * scale2 - m)
                pe = jnp.exp2(se * scale2 - m)
                total = jnp.sum(pp, axis=1, keepdims=True) + jnp.sum(pe, axis=1, keepdims=True)
                o = dot(pp.astype(BF16), vbuf[s, :, cols]) + dot(pe.astype(BF16), vext[s, :, cols])
                obuf[s, at, cols] = (o / total).astype(BF16)
                lses.append(m + jnp.log2(total))
            obuf[s, at, cw:] = pack_lse(lambda i: lses[i], blk).astype(BF16)
            return carry

        lax.fori_loop(0, nblk, block, 0)

    def send_c(s):
        src = obuf.at[s, pl.ds(pl.multiple_of((1 - core) * r1, r1), r1)]
        return remote(src, rc.at[s], scs.at[s], rcr.at[s], sib)

    def send_y(s):
        src = cbuf.at[s, pl.ds(pl.multiple_of((1 - y) * r2, r2), r2)]
        return remote(src, ry.at[s], sys_.at[s], ryr.at[s], ynb)

    def send_z(s, d):
        return remote(
            zbuf.at[s, lax.rem(z + d, nz)], rz.at[s, d - 1], szs.at[s, d - 1], rzr.at[s, d - 1],
            znb[d - 1],
        )

    def send_x(s, d):
        return remote(
            xbuf.at[s], rx.at[s, d - 1], sxs.at[s, d - 1], rxr.at[s, d - 1], xnb[d - 1]
        )

    def merge_c(s):
        send_c(s).wait_recv()
        mine = obuf[s, pl.ds(pl.multiple_of(core * r1, r1), r1), :]
        o, l = merge([mine, rc[s]])
        cbuf[s, :, 0:cw] = o.astype(BF16)
        cbuf[s, :, cw:] = pack_lse(lambda i: l[:, i * HD:(i + 1) * HD], r1).astype(BF16)
        send_y(s).start()

    piece = cw // fold

    def fold_rows(x):
        return jnp.concatenate([x[:, f * piece:(f + 1) * piece] for f in range(fold)], axis=0)

    def unfold_rows(x):
        return jnp.concatenate(
            [x[f * rc_rows:(f + 1) * rc_rows, 0:piece] for f in range(fold)], axis=1
        )

    def merge_y(s):
        send_y(s).wait_recv()
        mine = cbuf[s, pl.ds(pl.multiple_of(y * r2, r2), r2), :]
        o, l = merge([mine, ry[s]])
        packed = pack_lse(lambda i: l[:, i * HD:(i + 1) * HD], r2)
        for zz in range(nz):
            at = slice(zz * rc_rows, (zz + 1) * rc_rows)
            zbuf[s, zz, :, 0:piece] = fold_rows(o[at, :]).astype(BF16)
            zbuf[s, zz, :, piece:] = jnp.concatenate([packed[at, :]] * fold, axis=0).astype(BF16)
        for d in range(1, nz):
            send_z(s, d).start()

    def merge_z(s):
        parts = []
        for d in range(nz):
            if d:
                send_z(s, d).wait_recv()
                x = rz[s, d - 1].astype(F32)
            else:
                x = zbuf[s, z].astype(F32)
            parts.append(jnp.concatenate([unfold_rows(x), x[0:rc_rows, piece:]], axis=1))
        o, unused = merge(parts)
        xbuf[s] = fold_rows(o).astype(BF16)
        for d in range(1, g):
            send_x(s, d).start()

    def write(x, group, s):
        x = unfold_rows(x.astype(F32))
        mine = x[0:rows_slot]
        for p in range(1, g):
            mine = jnp.where(h == p, x[p * rows_slot:(p + 1) * rows_slot], mine)
        cols = pl.ds(pl.multiple_of(group * gw + s * cw, 128), cw)
        outa_ref[:, cols] = mine[0:tdev].astype(BF16)
        outb_ref[:, cols] = mine[tdev:rows_slot].astype(BF16)

    def turn(t, carry):
        @pl.when(t < steps)
        def _():
            compute(t)
            send_c(t).start()

        @pl.when((t >= 1) & (t < steps + 1))
        def _():
            merge_c(t - 1)

        @pl.when((t >= 2) & (t < steps + 2))
        def _():
            merge_y(t - 2)

        @pl.when(t >= 3)
        def _():
            merge_z(t - 3)

        return carry

    lax.fori_loop(0, steps + 3, turn, 0)

    def finish(s, carry):
        write(xbuf[s], h, s)
        for d in range(1, g):
            send_x(s, d).wait_recv()
            write(rx[s, d - 1], lax.rem(h + g - d, g), s)
            send_x(s, d).wait_send()
        send_c(s).wait_send()
        send_y(s).wait_send()
        for d in range(1, nz):
            send_z(s, d).wait_send()
        return carry

    lax.fori_loop(0, steps, finish, 0)
    for cp in gx + gz + [gy, gc]:
        cp.wait_send()


def local(
    response_input, response_queries, response_keys, response_values, prompt_keys, prompt_values,
    query_down_weight, query_up_weight, value_down_weight, value_up_weight, response_index,
):
    n = lax.axis_size("ctx")
    g = lax.axis_size("head")
    tdev, width = response_input.shape
    cache, gw = prompt_keys.shape
    chunks = 16 // tdev
    cjw = gw // chunks
    steps = chunks if cjw >= 256 else chunks // 2
    cw = gw // steps
    mw = cw + HD
    nz = n // 4
    ng = n * g
    rows = ng * 2 * tdev
    rc_rows = 2 * tdev * g
    fold = 1 if rc_rows >= 16 else 16 // rc_rows
    zr = rc_rows * fold
    extp = -(-2 * tdev * g // 16) * 16
    vmem = pl.BlockSpec(memory_space=pltpu.VMEM)
    hbm = pl.BlockSpec(memory_space=pl.ANY)
    dma = pltpu.SemaphoreType.DMA
    out = jax.ShapeDtypeStruct((tdev, width), BF16)
    return pl.pallas_call(
        functools.partial(kernel, n, g, tdev, steps),
        out_shape=(out, out),
        in_specs=[vmem, vmem, vmem, vmem, vmem, hbm, hbm, vmem, vmem, vmem, vmem],
        out_specs=(vmem, vmem),
        scratch_shapes=[
            pltpu.VMEM((16, cjw + HD), F32),
            pltpu.VMEM((g, 16, cjw + HD), BF16),
            pltpu.VMEM((g, 16, cjw), BF16),
            pltpu.VMEM((g, 16, cjw), BF16),
            pltpu.VMEM((ng, 16, cjw + HD), BF16),
            pltpu.VMEM((g, 16, cjw), BF16),
            pltpu.VMEM((g, 16, cjw), BF16),
            pltpu.VMEM((steps, cache, cw), BF16),
            pltpu.VMEM((steps, cache, cw), BF16),
            pltpu.VMEM((rows, extp), F32),
            pltpu.VMEM((steps, rows, cw), BF16),
            pltpu.VMEM((steps, extp, cw), BF16),
            pltpu.VMEM((steps, extp, cw), BF16),
            pltpu.VMEM((steps, rows, mw), BF16),
            pltpu.VMEM((steps, rows // 2, mw), BF16),
            pltpu.VMEM((steps, rows // 2, mw), BF16),
            pltpu.VMEM((steps, rows // 4, mw), BF16),
            pltpu.VMEM((steps, nz, zr, cw // fold + HD), BF16),
            pltpu.VMEM((steps, nz - 1, zr, cw // fold + HD), BF16),
            pltpu.VMEM((steps, zr, cw // fold), BF16),
            pltpu.VMEM((steps, g - 1, zr, cw // fold), BF16),
            dma((2, steps)),
            dma((g, 3)), dma((g, 3)), dma((nz,)), dma((nz,)),
            dma((1,)), dma((1,)), dma((1,)), dma((1,)),
            dma((steps,)), dma((steps,)), dma((steps,)), dma((steps,)),
            dma((steps, nz - 1)), dma((steps, nz - 1)),
            dma((steps, g - 1)), dma((steps, g - 1)),
        ],
        compiler_params=pltpu.CompilerParams(
            collective_id=0, has_side_effects=True, vmem_limit_bytes=60 * 1024 * 1024
        ),
    )(
        response_index.reshape(1, -1), response_input, response_queries, response_keys,
        response_values, prompt_keys, prompt_values, query_down_weight.T, query_up_weight,
        value_down_weight.T, value_up_weight,
    )


def solution(mesh):
    token = P(("ctx", "head"), None)
    return jax.shard_map(
        local,
        mesh=mesh,
        in_specs=(token, token, token, token, P("ctx", "head"), P("ctx", "head"))
        + (P(),) * 5,
        out_specs=(token, token),
        check_vma=False,
    )
```

```python
import functools

import jax
import jax.numpy as jnp
from jax import lax
from jax.experimental import pallas as pl
from jax.experimental.pallas import tpu as pltpu
from jax.sharding import PartitionSpec as P

HD = 128
LOG2E = 1.4426950408889634
F32 = jnp.float32
BF16 = jnp.bfloat16
MESH = pl.DeviceIdType.MESH


def dot(a, b):
    return jnp.dot(a, b, preferred_element_type=F32)


def dot_t(a, b):
    return lax.dot_general(a, b, (((1,), (1,)), ((), ())), preferred_element_type=F32)


def iota(shape, dim):
    return lax.broadcasted_iota(jnp.int32, shape, dim)


def vdiv(x, d):
    if d & (d - 1):
        return lax.div(x, d)
    return lax.shift_right_logical(x, jnp.int32(d.bit_length() - 1)) if d > 1 else x


def vrem(x, d):
    return lax.rem(x, d) if d & (d - 1) else x & (d - 1)


def kernel(
    n, g, tdev, steps,
    idx_ref, in_ref, q_ref, k_ref, v_ref, pk_hbm, pv_hbm, qd_ref, qu_ref, vd_ref, vu_ref,
    outa_ref, outb_ref,
    msgf, msg, kmsg, vmsg, gbuf, kx, vx, kbuf, vbuf, maskbuf, qbuf, kext, vext,
    obuf, rc, cbuf, ry, zbuf, rz, xbuf, rx, spread_ref,
    sem_kv, sx, rxs, sz, rzs, sy, rys, sc, rcs,
    scs, rcr, sys_, ryr, szs, rzr, sxs, rxr,
):
    c = lax.axis_index("ctx")
    h = lax.axis_index("head")
    nz = n // 4
    z = lax.div(c, 4)
    y = lax.rem(lax.div(c, 2), 2)
    core = lax.rem(c, 2)
    gw = pk_hbm.shape[1]
    chunks = 16 // tdev
    cjw = gw // chunks
    jper = chunks // steps
    cw = cjw * jper
    hc = cw // HD
    ng = n * g
    rows_slot = 2 * tdev
    rows = ng * rows_slot
    r1, r2 = rows // 2, rows // 4
    rc_rows = g * rows_slot
    fold = 1 if rc_rows >= 16 else 16 // rc_rows
    cache = pk_hbm.shape[0]
    blk = obuf.shape[1] if obuf.shape[1] < 128 else 128
    sb = blk // rows_slot
    nblk = rows // blk
    ext = g * rows_slot
    extp = kext.shape[1]
    tokens = ng * tdev

    def ctx_of(zz, yy, cc):
        return zz * 4 + yy * 2 + cc

    def slot_of(zz, yy, cc):
        return ((cc * 2 + yy) * nz + zz) * g

    def kv_copies(s):
        cols = pl.ds(s * cw, cw)
        return (
            pltpu.make_async_copy(pk_hbm.at[:, cols], kbuf.at[s], sem_kv.at[0, s]),
            pltpu.make_async_copy(pv_hbm.at[:, cols], vbuf.at[s], sem_kv.at[1, s]),
        )

    for s in range(steps):
        for cp in kv_copies(s):
            cp.start()

    barrier = pltpu.get_barrier_semaphore()
    sib = (ctx_of(z, y, 1 - core), h)
    ynb = (ctx_of(z, 1 - y, core), h)
    znb = [(ctx_of(lax.rem(z + d, nz), y, core), h) for d in range(1, nz)]
    xnb = [(c, lax.rem(h + d, g)) for d in range(1, g)]
    partners = [sib, ynb] + znb + xnb
    for p in partners:
        pl.semaphore_signal(barrier, inc=1, device_id=p, device_id_type=MESH)

    up_q = dot_t(in_ref[...], qd_ref[...])
    up_v = dot_t(in_ref[...], vd_ref[...])
    rank = up_q.shape[1]
    qf, kf, vf = (r[...].astype(F32) for r in (q_ref, k_ref, v_ref))
    msgf[...] = jnp.zeros(msgf.shape, F32)
    msgf[0:tdev, cjw:cjw + rank] = up_q
    msgf[tdev:2 * tdev, cjw:cjw + rank] = up_v
    for p in range(g):
        for src, dst in ((kf, kmsg), (vf, vmsg), (qf, msg)):
            for j in range(chunks):
                at = p * gw + j * cjw
                msgf[j * tdev:(j + 1) * tdev, 0:cjw] = src[:, at:at + cjw]
            if dst is msg:
                dst[p] = msgf[...].astype(BF16)
            else:
                dst[p] = msgf[:, 0:cjw].astype(BF16)

    pl.semaphore_wait(barrier, len(partners))

    my_slot = slot_of(z, y, core)

    def remote(src, dst, ss, rs, dev):
        return pltpu.make_async_remote_copy(
            src_ref=src, dst_ref=dst, send_sem=ss, recv_sem=rs, device_id=dev, device_id_type=MESH
        )

    gx = []
    for d in range(1, g):
        p = lax.rem(h + d, g)
        gx.append(remote(msg.at[p], gbuf.at[my_slot + h], sx.at[d, 0], rxs.at[d, 0], xnb[d - 1]))
        gx.append(remote(kmsg.at[p], kx.at[h], sx.at[d, 1], rxs.at[d, 1], xnb[d - 1]))
        gx.append(remote(vmsg.at[p], vx.at[h], sx.at[d, 2], rxs.at[d, 2], xnb[d - 1]))
    for cp in gx:
        cp.start()
    gbuf[my_slot + h] = msg[h]
    kx[h] = kmsg[h]
    vx[h] = vmsg[h]
    for cp in gx:
        cp.wait_recv()

    here = gbuf.at[pl.ds(my_slot, g)]
    gz = [remote(here, here, sz.at[d], rzs.at[d], znb[d - 1]) for d in range(1, nz)]
    for cp in gz:
        cp.start()
    gy, gc = [], []
    for d in range(nz):
        zs = lax.rem(z + nz - d, nz)
        part = gbuf.at[pl.ds(slot_of(zs, y, core), g)]
        gy.append(remote(part, part, sy.at[d], rys.at[d], ynb))
        gc.append(remote(part, part, sc.at[d], rcs.at[d], sib))
    for d in range(nz):
        zs = lax.rem(z + nz - d, nz)
        part = gbuf.at[pl.ds(slot_of(zs, 1 - y, core), g)]
        gc.append(remote(part, part, sc.at[nz + d], rcs.at[nz + d], sib))
    gy[0].start()
    gc[0].start()

    rr = iota((extp, g * 16), 0)
    rem = vrem(rr, g * tdev)
    ext_off = iota((extp, g * 16), 1) - (vdiv(rem, tdev) * 16 + vrem(rem, tdev))
    ext_off = jnp.where(rr < ext, ext_off, -1)

    def ext_select(j):
        return jnp.where(ext_off == j * tdev, 1.0, 0.0).astype(BF16)

    own = gbuf[pl.ds(my_slot, g)].reshape(g * 16, cjw + HD)
    av = dot(ext_select(1), own[:, cjw:])
    av = jnp.where(iota((extp, HD), 0) < g * tdev, av, 0.0).astype(BF16)[:, 0:rank]
    kxa = kx[...].reshape(g * 16, cjw)
    vxa = vx[...].reshape(g * 16, cjw)
    group_at = pl.multiple_of(h * gw, gw)
    for j in range(chunks):
        sel = ext_select(j)
        s, lo = j // jper, (j % jper) * cjw
        kext[s, :, lo:lo + cjw] = dot(sel, kxa).astype(BF16)
        wv = vu_ref[:, pl.ds(pl.multiple_of(group_at + j * cjw, 128), cjw)]
        vext[s, :, lo:lo + cjw] = (dot(sel, vxa) + dot(av, wv)).astype(BF16)

    rr = iota((blk, sb * 16), 0)
    q_off = iota((blk, sb * 16), 1) - (vdiv(rr, rows_slot) * 16 + vrem(rr, tdev))
    lane, col = iota((HD, cw), 0), iota((HD, cw), 1)
    e = (vrem(lane, hc) == vdiv(col, HD)) & (lane < 3 * hc)
    spread_ref[...] = jnp.where(e, 1.0, 0.0).astype(BF16)

    idx_row = idx_ref[...].astype(F32)
    eye = iota((tokens, tokens), 0) == iota((tokens, tokens), 1)
    idx_col = jnp.sum(jnp.where(eye, idx_row, 0.0), axis=1, keepdims=True)
    tok_u0 = c * (g * tdev) + vrem(iota((tokens, extp), 1), g * tdev)
    seg_u = jnp.sum(
        jnp.where(iota((tokens, extp), 0) == tok_u0, idx_col, 0.0), axis=0, keepdims=True
    )

    def row_tokens(shape, b):
        r = iota(shape, 0) + b * blk
        sl = vdiv(r, rows_slot)
        hh = vrem(sl, g)
        place = vdiv(sl, g)
        zz = vrem(place, nz)
        yc = vdiv(place, nz)
        ctx = zz * 4 + vrem(yc, 2) * 2 + vdiv(yc, 2)
        return (ctx * g + hh) * tdev + vrem(r, tdev), vrem(vdiv(r, tdev), 2)

    def mask_block(b, carry):
        tok_r, unused = row_tokens((blk, tokens), b)
        seg_r = jnp.sum(
            jnp.where(iota((blk, tokens), 1) == tok_r, idx_row, 0.0), axis=1, keepdims=True
        )
        tok, stream = row_tokens((blk, extp), b)
        u = iota((blk, extp), 1)
        tok_u = c * (g * tdev) + vrem(u, g * tdev)
        ok = (u < ext) & (vdiv(u, g * tdev) == stream) & (tok_u <= tok) & (seg_r == seg_u)
        maskbuf[pl.ds(pl.multiple_of(b * blk, blk), blk), :] = jnp.where(ok, 1.0, 0.0)
        return carry

    lax.fori_loop(0, nblk, mask_block, 0)

    for d in range(1, nz):
        gz[d - 1].wait_recv()
        gy[d].start()
        gc[d].start()
    for d in range(nz):
        gy[d].wait_recv()
        gc[nz + d].start()
    for cp in gc:
        cp.wait_recv()

    def q_select(j):
        return jnp.where(q_off == j * tdev, 1.0, 0.0).astype(BF16)

    def q_block(b, carry):
        x = gbuf[pl.ds(b * sb, sb)].reshape(sb * 16, cjw + HD)
        a = dot(q_select(0), x[:, cjw:])
        first = vrem(vdiv(iota((blk, HD), 0), tdev), 2) == 0
        a = jnp.where(first, a, 0.0).astype(BF16)[:, 0:rank]
        at = pl.ds(pl.multiple_of(b * blk, blk), blk)
        for j in range(chunks):
            wq = qu_ref[:, pl.ds(pl.multiple_of(group_at + j * cjw, 128), cjw)]
            s, lo = j // jper, (j % jper) * cjw
            qbuf[s, at, lo:lo + cjw] = (dot(q_select(j), x[:, 0:cjw]) + dot(a, wq)).astype(BF16)
        return carry

    lax.fori_loop(0, nblk, q_block, 0)

    scale2 = HD ** (-0.5) * LOG2E

    def pack_lse(cols_of, r):
        lane = iota((r, HD), 1)
        which = vrem(lane, hc)
        x = jnp.zeros((r, HD), F32)
        for i in range(hc):
            x = jnp.where(which == i, cols_of(i), x)
        hi = x.astype(BF16).astype(F32)
        mid = (x - hi).astype(BF16).astype(F32)
        lo = x - hi - mid
        x = jnp.where(lane < hc, hi, jnp.where(lane < 2 * hc, mid, lo))
        return jnp.where(lane < 3 * hc, x, 0.0)

    def spread(x):
        return dot(x.astype(BF16), spread_ref[...])

    def merge(parts):
        ls = [spread(p[:, cw:]) for p in parts]
        top = functools.reduce(jnp.maximum, ls)
        ws = [jnp.exp2(x - top) for x in ls]
        den = functools.reduce(jnp.add, ws)
        num = functools.reduce(jnp.add, [w * p[:, 0:cw].astype(F32) for w, p in zip(ws, parts)])
        return num / den, top + jnp.log2(den)

    def compute(s):
        for cp in kv_copies(s):
            cp.wait()

        def block(b, carry):
            at = pl.ds(pl.multiple_of(b * blk, blk), blk)
            seen = maskbuf[at, :] > 0.5
            lses = []
            for i in range(hc):
                cols = slice(i * HD, (i + 1) * HD)
                q = qbuf[s, at, cols]
                sp = dot_t(q, kbuf[s, :, cols])
                se = jnp.where(seen, dot_t(q, kext[s, :, cols]), -jnp.inf)
                m = jnp.maximum(
                    jnp.max(sp, axis=1, keepdims=True), jnp.max(se, axis=1, keepdims=True)
                ) * scale2
                pp = jnp.exp2(sp * scale2 - m)
                pe = jnp.exp2(se * scale2 - m)
                total = jnp.sum(pp, axis=1, keepdims=True) + jnp.sum(pe, axis=1, keepdims=True)
                o = dot(pp.astype(BF16), vbuf[s, :, cols]) + dot(pe.astype(BF16), vext[s, :, cols])
                obuf[s, at, cols] = (o / total).astype(BF16)
                lses.append(m + jnp.log2(total))
            obuf[s, at, cw:] = pack_lse(lambda i: lses[i], blk).astype(BF16)
            return carry

        lax.fori_loop(0, nblk, block, 0)

    def send_c(s):
        src = obuf.at[s, pl.ds(pl.multiple_of((1 - core) * r1, r1), r1)]
        return remote(src, rc.at[s], scs.at[s], rcr.at[s], sib)

    def send_y(s):
        src = cbuf.at[s, pl.ds(pl.multiple_of((1 - y) * r2, r2), r2)]
        return remote(src, ry.at[s], sys_.at[s], ryr.at[s], ynb)

    def send_z(s, d):
        return remote(
            zbuf.at[s, lax.rem(z + d, nz)], rz.at[s, d - 1], szs.at[s, d - 1], rzr.at[s, d - 1],
            znb[d - 1],
        )

    def send_x(s, d):
        return remote(
            xbuf.at[s], rx.at[s, d - 1], sxs.at[s, d - 1], rxr.at[s, d - 1], xnb[d - 1]
        )

    def merge_c(s):
        send_c(s).wait_recv()
        mine = obuf[s, pl.ds(pl.multiple_of(core * r1, r1), r1), :]
        o, l = merge([mine, rc[s]])
        cbuf[s, :, 0:cw] = o.astype(BF16)
        cbuf[s, :, cw:] = pack_lse(lambda i: l[:, i * HD:(i + 1) * HD], r1).astype(BF16)
        send_y(s).start()

    piece = cw // fold

    def fold_rows(x):
        return jnp.concatenate([x[:, f * piece:(f + 1) * piece] for f in range(fold)], axis=0)

    def unfold_rows(x):
        return jnp.concatenate(
            [x[f * rc_rows:(f + 1) * rc_rows, 0:piece] for f in range(fold)], axis=1
        )

    def merge_y(s):
        send_y(s).wait_recv()
        mine = cbuf[s, pl.ds(pl.multiple_of(y * r2, r2), r2), :]
        o, l = merge([mine, ry[s]])
        packed = pack_lse(lambda i: l[:, i * HD:(i + 1) * HD], r2)
        for zz in range(nz):
            at = slice(zz * rc_rows, (zz + 1) * rc_rows)
            zbuf[s, zz, :, 0:piece] = fold_rows(o[at, :]).astype(BF16)
            zbuf[s, zz, :, piece:] = jnp.concatenate([packed[at, :]] * fold, axis=0).astype(BF16)
        for d in range(1, nz):
            send_z(s, d).start()

    def merge_z(s):
        parts = []
        for d in range(nz):
            if d:
                send_z(s, d).wait_recv()
                x = rz[s, d - 1].astype(F32)
            else:
                x = zbuf[s, z].astype(F32)
            parts.append(jnp.concatenate([unfold_rows(x), x[0:rc_rows, piece:]], axis=1))
        o, unused = merge(parts)
        xbuf[s] = fold_rows(o).astype(BF16)
        for d in range(1, g):
            send_x(s, d).start()

    def write(x, group, s):
        x = unfold_rows(x.astype(F32))
        mine = x[0:rows_slot]
        for p in range(1, g):
            mine = jnp.where(h == p, x[p * rows_slot:(p + 1) * rows_slot], mine)
        cols = pl.ds(pl.multiple_of(group * gw + s * cw, 128), cw)
        outa_ref[:, cols] = mine[0:tdev].astype(BF16)
        outb_ref[:, cols] = mine[tdev:rows_slot].astype(BF16)

    def turn(t, carry):
        @pl.when(t < steps)
        def _():
            compute(t)
            send_c(t).start()

        @pl.when((t >= 1) & (t < steps + 1))
        def _():
            merge_c(t - 1)

        @pl.when((t >= 2) & (t < steps + 2))
        def _():
            merge_y(t - 2)

        @pl.when(t >= 3)
        def _():
            merge_z(t - 3)

        return carry

    lax.fori_loop(0, steps + 3, turn, 0)

    def finish(s, carry):
        write(xbuf[s], h, s)
        for d in range(1, g):
            send_x(s, d).wait_recv()
            write(rx[s, d - 1], lax.rem(h + g - d, g), s)
            send_x(s, d).wait_send()
        send_c(s).wait_send()
        send_y(s).wait_send()
        for d in range(1, nz):
            send_z(s, d).wait_send()
        return carry

    lax.fori_loop(0, steps, finish, 0)
    for cp in gx + gz + gy + gc:
        cp.wait_send()


def local(
    response_input, response_queries, response_keys, response_values, prompt_keys, prompt_values,
    query_down_weight, query_up_weight, value_down_weight, value_up_weight, response_index,
):
    n = lax.axis_size("ctx")
    g = lax.axis_size("head")
    tdev, width = response_input.shape
    cache, gw = prompt_keys.shape
    chunks = 16 // tdev
    cjw = gw // chunks
    steps = chunks // 2
    cw = gw // steps
    mw = cw + HD
    nz = n // 4
    ng = n * g
    rows = ng * 2 * tdev
    rc_rows = 2 * tdev * g
    fold = 1 if rc_rows >= 16 else 16 // rc_rows
    zr = rc_rows * fold
    extp = -(-2 * tdev * g // 16) * 16
    vmem = pl.BlockSpec(memory_space=pltpu.VMEM)
    hbm = pl.BlockSpec(memory_space=pl.ANY)
    dma = pltpu.SemaphoreType.DMA
    out = jax.ShapeDtypeStruct((tdev, width), BF16)
    return pl.pallas_call(
        functools.partial(kernel, n, g, tdev, steps),
        out_shape=(out, out),
        in_specs=[vmem, vmem, vmem, vmem, vmem, hbm, hbm, vmem, vmem, vmem, vmem],
        out_specs=(vmem, vmem),
        scratch_shapes=[
            pltpu.VMEM((16, cjw + HD), F32),
            pltpu.VMEM((g, 16, cjw + HD), BF16),
            pltpu.VMEM((g, 16, cjw), BF16),
            pltpu.VMEM((g, 16, cjw), BF16),
            pltpu.VMEM((ng, 16, cjw + HD), BF16),
            pltpu.VMEM((g, 16, cjw), BF16),
            pltpu.VMEM((g, 16, cjw), BF16),
            pltpu.VMEM((steps, cache, cw), BF16),
            pltpu.VMEM((steps, cache, cw), BF16),
            pltpu.VMEM((rows, extp), F32),
            pltpu.VMEM((steps, rows, cw), BF16),
            pltpu.VMEM((steps, extp, cw), BF16),
            pltpu.VMEM((steps, extp, cw), BF16),
            pltpu.VMEM((steps, rows, mw), BF16),
            pltpu.VMEM((steps, rows // 2, mw), BF16),
            pltpu.VMEM((steps, rows // 2, mw), BF16),
            pltpu.VMEM((steps, rows // 4, mw), BF16),
            pltpu.VMEM((steps, nz, zr, cw // fold + HD), BF16),
            pltpu.VMEM((steps, nz - 1, zr, cw // fold + HD), BF16),
            pltpu.VMEM((steps, zr, cw // fold), BF16),
            pltpu.VMEM((steps, g - 1, zr, cw // fold), BF16),
            pltpu.VMEM((HD, cw), BF16),
            dma((2, steps)),
            dma((g, 3)), dma((g, 3)), dma((nz,)), dma((nz,)),
            dma((nz,)), dma((nz,)), dma((2 * nz,)), dma((2 * nz,)),
            dma((steps,)), dma((steps,)), dma((steps,)), dma((steps,)),
            dma((steps, nz - 1)), dma((steps, nz - 1)),
            dma((steps, g - 1)), dma((steps, g - 1)),
        ],
        compiler_params=pltpu.CompilerParams(
            collective_id=0, has_side_effects=True, vmem_limit_bytes=60 * 1024 * 1024
        ),
    )(
        response_index.reshape(1, -1), response_input, response_queries, response_keys,
        response_values, prompt_keys, prompt_values, query_down_weight.T, query_up_weight,
        value_down_weight.T, value_up_weight,
    )


def solution(mesh):
    token = P(("ctx", "head"), None)
    return jax.shard_map(
        local,
        mesh=mesh,
        in_specs=(token, token, token, token, P("ctx", "head"), P("ctx", "head"))
        + (P(),) * 5,
        out_specs=(token, token),
        check_vma=False,
    )
```
